32 devices in a mesh: seq: 16 (over z, y, x), dp: 2 (over core).
Axes of the slice: x: 2, y: 2, z: 4, core: 2. Of those that a mesh axis runs over, the one named last changes fastest.
Arguments:
- queries: bfloat16 [32768, 768], P(('dp', 'seq')), parts along dimension 0, may hold values from -2.5 to 2.5
- keys: bfloat16 [32768, 768], P(('dp', 'seq')), parts along dimension 0, may hold values from -2.5 to 2.5
- values: bfloat16 [32768, 768], P(('dp', 'seq')), parts along dimension 0, may hold values from -6 to 6
- norm_gain: float32 [768], replicated, may hold values from 0.5 to 1.5
- expert_ids: int32 [32768, 1], P(('dp', 'seq')), parts along dimension 0, may hold values from 0 to 31; in each aligned block of 1024 rows (0 to 1023, 1024 to 2047, ...) at most 48 rows name the same one
- w_in: bfloat16 [64, 768, 3072], P(('dp', 'seq')), parts along dimension 0, may hold values from -0.21875 to 0.21875
- w_out: bfloat16 [64, 3072, 768], P(('dp', 'seq')), parts along dimension 0, may hold values from -0.109375 to 0.109375
Outputs:
- block_output: bfloat16 [32768, 768], P(('dp', 'seq')), parts along dimension 0
The draws below stay inside these ranges and needn't reach their ends.
There are 2 independent parts, one for each index of `dp`. The reference program is written for one: setup_inputs(seed, part) draws one part's arguments, and reference() takes and returns one part's arrays. A program takes and returns all parts, laid end to end along the dimension named above; an argument that names none is the same for every part. Nothing has to cross between parts.
Inputs may be any that keep to these rules, and one draw needn't show every extreme that they name: `expert_ids`: within each aligned block of 1024 rows no expert is named more than 48 times, and in every draw some expert is named exactly 48 times in some block.
All inputs are finite; a program needn't handle non-finite values.
Results may differ from the reference program's by a relative error of at most 0.008.
Values may be sent and summed in bfloat16 or wider, within the bound.
No kernel may reach another device: no remote copies, remote signals or barrier semaphores. Data moves between devices by JAX's collectives and lax.ppermute only.
A program may use at most 128 MiB of HBM per device.

```python
import math
import jax
import jax.numpy as jnp
import numpy as np
from jax import lax

HEADS = 12
D = 768
FF = 3072
EXPERTS = 32
TOK_DEV = 1024
TOKENS = 16384
CAP = 48
N_SEQ = 16


def block_levels(rng, extent, cuts, smallest, largest):
    gain, own = 1.0, jax.random.fold_in(rng, 6)
    for position, blocks in cuts:
        draws = jnp.exp(jax.random.uniform(jax.random.fold_in(own, position), (blocks,), jnp.float32, smallest / len(cuts), largest / len(cuts)))
        gain = gain * jnp.repeat(draws, extent[position] // blocks).reshape([-1 if axis == position else 1 for axis in range(len(extent))])
    return gain


def routed_block(key, own, number, rows, number_of, top, bound, slope):
    sequence = jax.random.permutation(key, number_of)
    crowded, usual = load_shares(number_of, rows * top, bound, slope, True), load_shares(number_of, rows * top, bound, slope, False)
    places = jnp.arange(number_of)

    def named(sizes, offset_by):
        used = int((sizes > 0).sum())
        fixed = max(1, used // 4)
        passed = fixed + (places - fixed + offset_by * (used - fixed)) % max(1, number_of - fixed)
        return jnp.zeros((number_of,), jnp.int32).at[sequence[jnp.where(places < fixed, places, passed)]].set(jnp.asarray(sizes, jnp.int32))

    sizes = jnp.where(number % 4 == 0, named(crowded, number // 4), named(usual, number - number // 4 - 1))
    mixed = jax.random.permutation(jax.random.fold_in(own, 3), number_of)
    giver, receiver = mixed[0:number_of // 2 * 2:2], mixed[1:number_of // 2 * 2:2]
    margin = jnp.minimum(sizes[giver] - 1, bound - sizes[receiver]) // 2
    margin = jnp.where((giver == sequence[0]) | (receiver == sequence[0]) | (sizes[receiver] == 0), 0, jnp.maximum(margin, 0))
    passed = jax.random.randint(jax.random.fold_in(own, 4), (number_of // 2,), 0, 1 << 20) % (margin + 1)
    sizes = sizes.at[giver].add(-passed).at[receiver].add(passed)
    labels = jnp.searchsorted(jnp.cumsum(sizes), jnp.arange(rows * top), side="right").astype(jnp.int32)
    grid = labels.reshape(top, rows).T
    grid = grid[jax.random.permutation(jax.random.fold_in(own, 1), rows)]
    offset_by = jax.random.randint(jax.random.fold_in(own, 2), (rows, 1), 0, top)
    return jnp.take_along_axis(grid, (jnp.arange(top)[None, :] + offset_by) % top, axis=1)


def load_shares(count, total, most, lean, full):
    portions = [(1 << 20) // math.isqrt(standing ** lean) + 1 for standing in range(1, count + 1)]
    largest = most if full else min(most, max(-(-total // count), total * portions[0] // sum(portions)))
    least = 1 if total - largest >= count - 1 else 0
    given, surplus = [largest] + [least] * (count - 1), total - largest - least * (count - 1)
    while surplus > 0:
        candidates = [i for i in range(1, count) if given[i] < largest] or [i for i in range(1, count) if given[i] < most]
        mass, budget = sum([portions[i] for i in candidates]), surplus
        for i in candidates:
            addition = min(most - given[i], max(1, budget * portions[i] // mass), surplus)
            given[i] = given[i] + addition
            surplus = surplus - addition
    return np.array(given)


def gaussian(own_key, shape, width, most, cuts=(), kind=jnp.bfloat16):
    result = width * jax.random.normal(own_key, shape, jnp.float32)
    if cuts:
        result = result * block_levels(own_key, shape, cuts, -0.22, 0.18)
    return jnp.clip(result, -most, most).astype(kind)


def setup_inputs(seed: int = 0, part: int = 0) -> dict:
    streams_of = jax.random.split(jax.random.key(seed), 8)
    part_keys = jax.random.split(jax.random.fold_in(streams_of[7], part), 8)
    queries = gaussian(part_keys[0], (TOKENS, D), 0.35, 2.5, ((0, 16),))
    keys = gaussian(part_keys[1], (TOKENS, D), 0.35, 2.5, ((0, 16),))
    values = gaussian(part_keys[2], (TOKENS, D), 1.0, 6.0, ((0, 16),))
    norm_gain = jnp.clip(1.0 + 0.1 * jax.random.normal(streams_of[3], (D,), jnp.float32), 0.5, 1.5)
    expert_ids_keys = jax.random.split(jax.random.fold_in(part_keys[4], 1), TOKENS // TOK_DEV)
    expert_ids_turns = jax.random.permutation(jax.random.fold_in(part_keys[4], 3), TOKENS // TOK_DEV)
    expert_ids = jax.vmap(lambda own, number: routed_block(jax.random.fold_in(part_keys[4], 2), own, number, TOK_DEV, EXPERTS, 1, CAP, 2))(expert_ids_keys, expert_ids_turns).reshape((TOKENS, 1))
    w_in = gaussian(part_keys[5], (EXPERTS, D, FF), D ** -0.5, 0.21875, ((0, 16),))
    w_out = gaussian(part_keys[6], (EXPERTS, FF, D), FF ** -0.5, 0.109375, ((0, 16),))
    return {"queries": queries, "keys": keys, "values": values, "norm_gain": norm_gain, "expert_ids": expert_ids, "w_in": w_in, "w_out": w_out}


epsilon = 1e-06

def attend(queries, keys, values):
    head_width = D // HEADS
    query_blocks = queries.reshape(N_SEQ, TOK_DEV, HEADS, head_width)
    key_blocks = keys.reshape(N_SEQ, TOK_DEV, HEADS, head_width)
    value_blocks = values.reshape(N_SEQ, TOK_DEV, HEADS, head_width)
    causal = jnp.arange(TOK_DEV)[:, None] >= jnp.arange(TOK_DEV)[None, :]

    def one_block(carried, blocks):
        query_heads, key_heads, value_heads = blocks
        scores = jnp.einsum('thd,shd->hts', query_heads.astype(jnp.float32), key_heads.astype(jnp.float32))
        scores = jnp.where(causal[None], scores, 0.0).astype(jnp.bfloat16)
        local_part = jnp.einsum('hts,shd->thd', scores.astype(jnp.float32), value_heads.astype(jnp.float32))
        carried_part = jnp.einsum('thd,hde->the', query_heads.astype(jnp.float32), carried, precision=lax.Precision.HIGHEST)
        block_state = jnp.einsum('thd,the->hde', key_heads.astype(jnp.float32), value_heads.astype(jnp.float32))
        return (carried + block_state, local_part + carried_part)
    start_state = jnp.zeros((HEADS, head_width, head_width), jnp.float32)
    final_state, mixed = lax.scan(one_block, start_state, (query_blocks, key_blocks, value_blocks))
    return mixed.reshape(TOKENS, D)

def reference(queries, keys, values, norm_gain, expert_ids, w_in, w_out):
    mixed = attend(queries, keys, values)
    scale = lax.rsqrt(lax.optimization_barrier(jnp.mean(mixed * mixed, axis=-1, keepdims=True)) + epsilon)
    normed = (mixed * scale * norm_gain).astype(jnp.bfloat16)
    routes = expert_ids[:, 0].astype(jnp.int32)
    sort_order = jnp.argsort(routes, stable=True).astype(jnp.int32)
    expert_counts = jnp.zeros((EXPERTS,), jnp.int32).at[routes].add(1)
    expert_starts = (jnp.cumsum(expert_counts) - expert_counts).astype(jnp.int32)
    window = N_SEQ * CAP
    padded_rows = jnp.concatenate([normed[sort_order], jnp.zeros((window, D), jnp.bfloat16)], axis=0)

    def run_expert(expert_index):
        window_rows = lax.dynamic_slice(padded_rows, (expert_starts[expert_index], jnp.int32(0)), (window, D))
        hidden = jnp.dot(window_rows, w_in[expert_index], preferred_element_type=jnp.float32)
        hidden = jnp.maximum(hidden, 0.0).astype(jnp.bfloat16)
        return jnp.dot(hidden, w_out[expert_index], preferred_element_type=jnp.float32).astype(jnp.bfloat16)
    expert_rows = lax.map(run_expert, jnp.arange(EXPERTS, dtype=jnp.int32))
    sorted_routes = routes[sort_order]
    slot_rank = (jnp.arange(TOKENS, dtype=jnp.int32) - expert_starts[sorted_routes]).astype(jnp.int32)
    sorted_out = expert_rows[sorted_routes, slot_rank]
    expert_out = jnp.zeros((TOKENS, D), jnp.bfloat16).at[sort_order].set(sorted_out)
    return (normed.astype(jnp.float32) + expert_out.astype(jnp.float32)).astype(jnp.bfloat16)
```

```python
import functools

import jax
import jax.numpy as jnp
from jax import lax
from jax.experimental import pallas as pl
from jax.experimental.pallas import tpu as pltpu
from jax.sharding import PartitionSpec as P

HEADS = 12
RADIX = 4
MIB = 1 << 20

epsilon = 1e-06


def tile_of(extent, most):
    tile = min(extent, most)
    while extent % tile:
        tile -= 1
    return tile


def head_of_lane(shape, head_width):
    return lax.broadcasted_iota(jnp.int32, shape, 1) // head_width


def spread(compact, head_width):
    lanes = compact.shape[1]
    heads = lanes // head_width
    own = head_of_lane(compact.shape, head_width)
    return jnp.concatenate(
        [jnp.where(own == head, compact, jnp.zeros_like(compact)) for head in range(heads)], axis=0
    )


def gather_diagonal(square, head_width):
    lanes = square.shape[1]
    own = head_of_lane((head_width, lanes), head_width)
    total = jnp.zeros((head_width, lanes), square.dtype)
    for head in range(lanes // head_width):
        part = square[head * head_width : (head + 1) * head_width]
        total = total + jnp.where(own == head, part, 0.0)
    return total


def transposed_dot(left, right):
    return lax.dot_general(left, right, (((0,), (0,)), ((), ())), preferred_element_type=jnp.float32)


def state_kernel(head_width, keys, values, state):
    square = transposed_dot(keys[...], values[...])
    state[...] = gather_diagonal(square, head_width)


def block_states(keys, values, head_width, lanes):
    rows, width = keys.shape
    return pl.pallas_call(
        functools.partial(state_kernel, head_width),
        grid=(width // lanes,),
        in_specs=[pl.BlockSpec((rows, lanes), lambda g: (0, g))] * 2,
        out_specs=pl.BlockSpec((head_width, lanes), lambda g: (0, g)),
        out_shape=jax.ShapeDtypeStruct((head_width, width), jnp.float32),
        cost_estimate=pl.CostEstimate(flops=2 * rows * width * lanes, bytes_accessed=4 * rows * width, transcendentals=0),
        name="block_state",
    )(keys, values)


def local_kernel(head_width, queries, keys, values, mixed, state):
    chunk = pl.program_id(1)

    @pl.when(chunk == 0)
    def _():
        state[...] = jnp.zeros_like(state)

    query, key, value = queries[...], keys[...], values[...]
    rows, lanes = query.shape
    own = head_of_lane((rows, lanes), head_width)
    causal = lax.broadcasted_iota(jnp.int32, (rows, rows), 0) >= lax.broadcasted_iota(jnp.int32, (rows, rows), 1)
    total = jnp.dot(query, spread(state[...], head_width).astype(jnp.bfloat16), preferred_element_type=jnp.float32)
    for head in range(lanes // head_width):
        chosen = own == head
        scores = lax.dot_general(
            jnp.where(chosen, query, jnp.zeros_like(query)),
            key,
            (((1,), (1,)), ((), ())),
            preferred_element_type=jnp.float32,
        )
        scores = jnp.where(causal, scores, 0.0).astype(jnp.bfloat16)
        total = total + jnp.dot(
            scores, jnp.where(chosen, value, jnp.zeros_like(value)), preferred_element_type=jnp.float32
        )
    mixed[...] = total
    state[...] += gather_diagonal(transposed_dot(key, value), head_width)


def local_attention(queries, keys, values, head_width, lanes):
    rows, width = queries.shape
    chunk = tile_of(rows, 256)
    spec = pl.BlockSpec((chunk, lanes), lambda g, c: (c, g))
    return pl.pallas_call(
        functools.partial(local_kernel, head_width),
        grid=(width // lanes, rows // chunk),
        in_specs=[spec] * 3,
        out_specs=spec,
        out_shape=jax.ShapeDtypeStruct((rows, width), jnp.float32),
        scratch_shapes=[pltpu.VMEM((head_width, lanes), jnp.float32)],
        cost_estimate=pl.CostEstimate(
            flops=20 * rows * width * lanes, bytes_accessed=10 * rows * width, transcendentals=0
        ),
        name="local_attention",
    )(queries, keys, values)


def route_kernel(experts, capacity, per_device, ids_column, ids_row, slots_column, slots_row):
    rows = ids_column.shape[0]
    one, zero = jnp.float32(1.0), jnp.float32(0.0)
    before = lax.broadcasted_iota(jnp.int32, (rows, rows), 0) >= lax.broadcasted_iota(jnp.int32, (rows, rows), 1)
    after = lax.broadcasted_iota(jnp.int32, (rows, rows), 0) <= lax.broadcasted_iota(jnp.int32, (rows, rows), 1)
    lower = jnp.where(before, one, zero).astype(jnp.bfloat16)
    upper = jnp.where(after, one, zero).astype(jnp.bfloat16)

    def place(ids, matches, running, axis):
        rank = jnp.sum(matches * running, axis=axis, keepdims=True) - 1.0
        return (ids % per_device) * (experts // per_device) * capacity + (ids // per_device) * capacity + rank.astype(jnp.int32)

    column = ids_column[...]
    matches = jnp.where(column == lax.broadcasted_iota(jnp.int32, (rows, experts), 1), one, zero)
    running = jnp.dot(lower, matches.astype(jnp.bfloat16), preferred_element_type=jnp.float32)
    slots_column[...] = place(column, matches, running, 1)
    row = ids_row[...]
    matches = jnp.where(row == lax.broadcasted_iota(jnp.int32, (experts, rows), 0), one, zero)
    running = jnp.dot(matches.astype(jnp.bfloat16), upper, preferred_element_type=jnp.float32)
    slots_row[...] = place(row, matches, running, 0)


def route(expert_ids, experts, capacity, per_device):
    rows = expert_ids.shape[0]
    return pl.pallas_call(
        functools.partial(route_kernel, experts, capacity, per_device),
        grid=(1,),
        in_specs=[pl.BlockSpec((rows, 1), lambda i: (0, 0)), pl.BlockSpec((1, rows), lambda i: (0, 0))],
        out_specs=[pl.BlockSpec((rows, 1), lambda i: (0, 0)), pl.BlockSpec((1, rows), lambda i: (0, 0))],
        out_shape=[jax.ShapeDtypeStruct((rows, 1), jnp.int32), jax.ShapeDtypeStruct((1, rows), jnp.int32)],
        compiler_params=pltpu.CompilerParams(vmem_limit_bytes=32 * MIB),
        cost_estimate=pl.CostEstimate(flops=4 * rows * rows * experts, bytes_accessed=16 * rows, transcendentals=0),
        name="route",
    )(expert_ids, expert_ids.reshape(1, rows))


def earlier_states(state):
    size = lax.axis_size("seq")
    me = lax.axis_index("seq")
    prefix = jnp.zeros_like(state)
    total = state
    reach = 1
    while reach < size:
        radix = min(RADIX, size // reach)
        digit = (me // reach) % radix
        sent = total.astype(jnp.bfloat16)
        gained = jnp.zeros_like(state)
        lower = jnp.zeros_like(state)
        for step in range(1, radix):
            pairs = [(i, i + ((((i // reach) % radix) ^ step) - (i // reach) % radix) * reach) for i in range(size)]
            got = lax.ppermute(sent, "seq", pairs).astype(jnp.float32)
            gained = gained + got
            lower = lower + jnp.where((digit ^ step) < digit, got, 0.0)
        prefix = prefix + lower
        total = total + gained
        reach *= radix
    return prefix


def send_kernel(head_width, lanes, chunks, tiles, queries, mixed, carried, gain, slots, normed, *rest):
    outs, held = rest[:-1], rest[-1]
    step = pl.program_id(0)

    @pl.when(step < chunks)
    def _():
        rows, width = queries.shape
        query = queries[...]
        parts = []
        square = jnp.zeros((rows, 1), jnp.float32)
        for group in range(width // lanes):
            at = slice(group * lanes, (group + 1) * lanes)
            moved = spread(carried[:, at], head_width).astype(jnp.bfloat16)
            part = mixed[:, at] + jnp.dot(query[:, at], moved, preferred_element_type=jnp.float32)
            square = square + jnp.sum(part * part, axis=1, keepdims=True)
            parts.append(part)
        scale = lax.rsqrt(square / width + epsilon)
        start = pl.multiple_of(step * rows, rows)
        for group, part in enumerate(parts):
            at = slice(group * lanes, (group + 1) * lanes)
            final = (part * scale * gain[:, at]).astype(jnp.bfloat16)
            normed[:, at] = final
            held[pl.ds(start, rows), at] = final

    for index, out in enumerate(outs):
        first = chunks + index * tiles

        @pl.when((step >= first) & (step < first + tiles))
        def _(out=out):
            size = out.shape[0]
            place = (step - chunks) * size + lax.broadcasted_iota(jnp.int32, (size, held.shape[0]), 0)
            chosen = jnp.where(place == slots[...], 1.0, 0.0).astype(jnp.bfloat16)
            out[...] = jnp.dot(chosen, held[...], preferred_element_type=jnp.float32).astype(jnp.bfloat16)


def norm_and_sort(queries, mixed, carried, gain, slots, slot_count, arrays, head_width, lanes):
    rows, width = queries.shape
    chunk = tile_of(rows, 256)
    chunks = rows // chunk
    share = slot_count // arrays
    tile = tile_of(share, 256)
    tiles = share // tile
    by_chunk = pl.BlockSpec((chunk, width), lambda i: (jnp.minimum(i, chunks - 1), 0))

    def whole(shape):
        return pl.BlockSpec(shape, lambda i: (0, 0))

    def out_spec(index):
        return pl.BlockSpec((tile, width), lambda i: (jnp.clip(i - chunks - index * tiles, 0, tiles - 1), 0))

    return pl.pallas_call(
        functools.partial(send_kernel, head_width, lanes, chunks, tiles),
        grid=(chunks + arrays * tiles,),
        in_specs=[by_chunk, by_chunk, whole(carried.shape), whole(gain.shape), whole(slots.shape)],
        out_specs=[by_chunk] + [out_spec(index) for index in range(arrays)],
        out_shape=[jax.ShapeDtypeStruct((rows, width), jnp.bfloat16)]
        + [jax.ShapeDtypeStruct((share, width), jnp.bfloat16)] * arrays,
        scratch_shapes=[pltpu.VMEM((rows, width), jnp.bfloat16)],
        compiler_params=pltpu.CompilerParams(vmem_limit_bytes=32 * MIB),
        cost_estimate=pl.CostEstimate(
            flops=2 * rows * width * (slot_count + lanes), bytes_accessed=12 * rows * width, transcendentals=0
        ),
        name="norm_and_sort",
    )(queries, mixed, carried, gain, slots)


def expert_kernel(rows_ref, first, second, out, total):
    step = pl.program_id(0)
    hidden = jnp.dot(rows_ref[...], first[0], preferred_element_type=jnp.float32)
    hidden = jnp.maximum(hidden, 0.0).astype(jnp.bfloat16)
    added = jnp.dot(hidden, second[0], preferred_element_type=jnp.float32)

    @pl.when(step == 0)
    def _():
        total[...] = added

    @pl.when(step > 0)
    def _():
        total[...] += added

    @pl.when(step == pl.num_programs(0) - 1)
    def _():
        out[...] = total[...].astype(jnp.bfloat16)


def run_expert(arrived, w_in, w_out, expert):
    rows, width = arrived.shape
    hidden = w_in.shape[2]
    tile = tile_of(hidden, 768)
    return pl.pallas_call(
        expert_kernel,
        grid=(hidden // tile,),
        in_specs=[
            pl.BlockSpec((rows, width), lambda f: (0, 0)),
            pl.BlockSpec((1, width, tile), lambda f: (expert, 0, f)),
            pl.BlockSpec((1, tile, width), lambda f: (expert, f, 0)),
        ],
        out_specs=pl.BlockSpec((rows, width), lambda f: (0, 0)),
        out_shape=jax.ShapeDtypeStruct((rows, width), jnp.bfloat16),
        scratch_shapes=[pltpu.VMEM((rows, width), jnp.float32)],
        compiler_params=pltpu.CompilerParams(vmem_limit_bytes=40 * MIB),
        cost_estimate=pl.CostEstimate(
            flops=4 * rows * width * hidden, bytes_accessed=4 * width * (rows + hidden), transcendentals=0
        ),
        name="expert",
    )(arrived, w_in, w_out)


def combine_kernel(first_slot, base, returned, slots, out):
    place = first_slot + lax.broadcasted_iota(jnp.int32, (base.shape[0], returned.shape[0]), 1)
    chosen = jnp.where(place == slots[...], 1.0, 0.0).astype(jnp.bfloat16)
    moved = jnp.dot(chosen, returned[...], preferred_element_type=jnp.float32)
    out[...] = (base[...].astype(jnp.float32) + moved).astype(jnp.bfloat16)


def combine(base, returned, slots, first_slot):
    rows, width = base.shape
    chunk = tile_of(rows, 256)
    return pl.pallas_call(
        functools.partial(combine_kernel, first_slot),
        grid=(rows // chunk,),
        in_specs=[
            pl.BlockSpec((chunk, width), lambda i: (i, 0)),
            pl.BlockSpec(returned.shape, lambda i: (0, 0)),
            pl.BlockSpec((chunk, 1), lambda i: (i, 0)),
        ],
        out_specs=pl.BlockSpec((chunk, width), lambda i: (i, 0)),
        out_shape=jax.ShapeDtypeStruct((rows, width), jnp.bfloat16),
        compiler_params=pltpu.CompilerParams(vmem_limit_bytes=32 * MIB),
        cost_estimate=pl.CostEstimate(
            flops=2 * rows * width * returned.shape[0], bytes_accessed=8 * rows * width, transcendentals=0
        ),
        name="combine",
    )(base, returned, slots)


def shards(queries, keys, values, norm_gain, expert_ids, w_in, w_out):
    rows, width = queries.shape
    head_width = width // HEADS
    lanes = head_width * tile_of(HEADS, max(1, 256 // head_width))
    seq_count = lax.axis_size("seq")
    per_device = w_in.shape[0]
    experts = per_device * seq_count
    capacity = max(2, 3 * rows // (2 * experts))
    state = block_states(keys, values, head_width, lanes)
    carried = earlier_states(state)
    mixed = local_attention(queries, keys, values, head_width, lanes)
    slots_column, slots_row = route(expert_ids, experts, capacity, per_device)
    normed, *outgoing = norm_and_sort(
        queries, mixed, carried, norm_gain.reshape(1, width), slots_row, experts * capacity, per_device, head_width, lanes
    )

    def exchange(array):
        array = array.reshape(seq_count, capacity, width)
        return lax.all_to_all(array, "seq", split_axis=0, concat_axis=0, tiled=True).reshape(seq_count * capacity, width)

    arrived = [exchange(array) for array in outgoing]
    finished = [run_expert(array, w_in, w_out, expert) for expert, array in enumerate(arrived)]
    returned = [exchange(array) for array in finished]
    out = normed
    for expert, array in enumerate(returned):
        out = combine(out, array, slots_column, expert * seq_count * capacity)
    return out


def solution(mesh):
    in_specs = (
        P(("dp", "seq"), None),
        P(("dp", "seq"), None),
        P(("dp", "seq"), None),
        P(),
        P(("dp", "seq"), None),
        P(("dp", "seq"), None, None),
        P(("dp", "seq"), None, None),
    )
    out_specs = P(("dp", "seq"), None)
    return jax.shard_map(shards, mesh=mesh, in_specs=in_specs, out_specs=out_specs, check_vma=False)
```

```python
import functools

import jax
import jax.numpy as jnp
from jax import lax
from jax.experimental import pallas as pl
from jax.experimental.pallas import tpu as pltpu
from jax.sharding import PartitionSpec as P

HEADS = 12
RADIX = 4
MIB = 1 << 20
ANY = pl.BlockSpec(memory_space=pl.ANY)

epsilon = 1e-06


def tile_of(extent, most):
    tile = min(extent, most)
    while extent % tile:
        tile -= 1
    return tile


def head_of_lane(shape, head_width):
    return lax.broadcasted_iota(jnp.int32, shape, 1) // head_width


def spread(compact, head_width):
    lanes = compact.shape[1]
    heads = lanes // head_width
    own = head_of_lane(compact.shape, head_width)
    return jnp.concatenate(
        [jnp.where(own == head, compact, jnp.zeros_like(compact)) for head in range(heads)], axis=0
    )


def gather_diagonal(square, head_width):
    lanes = square.shape[1]
    own = head_of_lane((head_width, lanes), head_width)
    total = jnp.zeros((head_width, lanes), square.dtype)
    for head in range(lanes // head_width):
        part = square[head * head_width : (head + 1) * head_width]
        total = total + jnp.where(own == head, part, 0.0)
    return total


def transposed_dot(left, right):
    return lax.dot_general(left, right, (((0,), (0,)), ((), ())), preferred_element_type=jnp.float32)


def state_kernel(head_width, lanes, keys, values, state, sent):
    step = pl.program_id(0)

    @pl.when(step == 0)
    def _():
        state[...] = jnp.zeros_like(state)

    for start in range(0, keys.shape[1], lanes):
        at = slice(start, start + lanes)
        state[:, at] += gather_diagonal(transposed_dot(keys[:, at], values[:, at]), head_width)

    @pl.when(step == pl.num_programs(0) - 1)
    def _():
        sent[...] = state[...].astype(jnp.bfloat16)


def block_states(keys, values, head_width, lanes):
    rows, width = keys.shape
    chunk = tile_of(rows, 512)
    return pl.pallas_call(
        functools.partial(state_kernel, head_width, lanes),
        grid=(rows // chunk,),
        in_specs=[pl.BlockSpec((chunk, width), lambda c: (c, 0))] * 2,
        out_specs=[pl.BlockSpec((head_width, width), lambda c: (0, 0))] * 2,
        out_shape=[
            jax.ShapeDtypeStruct((head_width, width), jnp.float32),
            jax.ShapeDtypeStruct((head_width, width), jnp.bfloat16),
        ],
        cost_estimate=pl.CostEstimate(flops=2 * rows * width * lanes, bytes_accessed=4 * rows * width, transcendentals=0),
        name="block_state",
    )(keys, values)


def local_kernel(head_width, chunk, queries, keys, values, mixed):
    rows, lanes = queries.shape
    own = head_of_lane((chunk, lanes), head_width)
    causal = lax.broadcasted_iota(jnp.int32, (chunk, chunk), 0) >= lax.broadcasted_iota(jnp.int32, (chunk, chunk), 1)
    state = None
    for start in range(0, rows, chunk):
        at = slice(start, start + chunk)
        query, key, value = queries[at], keys[at], values[at]
        total = jnp.zeros((chunk, lanes), jnp.float32)
        if state is not None:
            total = jnp.dot(query, spread(state, head_width).astype(jnp.bfloat16), preferred_element_type=jnp.float32)
        for head in range(lanes // head_width):
            chosen = own == head
            scores = lax.dot_general(
                jnp.where(chosen, query, jnp.zeros_like(query)),
                key,
                (((1,), (1,)), ((), ())),
                preferred_element_type=jnp.float32,
            )
            scores = jnp.where(causal, scores, 0.0).astype(jnp.bfloat16)
            total = total + jnp.dot(
                scores, jnp.where(chosen, value, jnp.zeros_like(value)), preferred_element_type=jnp.float32
            )
        mixed[at] = total
        if start + chunk < rows:
            added = gather_diagonal(transposed_dot(key, value), head_width)
            state = added if state is None else state + added


def local_attention(queries, keys, values, head_width, lanes):
    rows, width = queries.shape
    chunk = tile_of(rows, 256)
    spec = pl.BlockSpec((rows, lanes), lambda g: (0, g))
    return pl.pallas_call(
        functools.partial(local_kernel, head_width, chunk),
        grid=(width // lanes,),
        in_specs=[spec] * 3,
        out_specs=spec,
        out_shape=jax.ShapeDtypeStruct((rows, width), jnp.float32),
        compiler_params=pltpu.CompilerParams(vmem_limit_bytes=32 * MIB),
        cost_estimate=pl.CostEstimate(
            flops=20 * rows * width * lanes, bytes_accessed=10 * rows * width, transcendentals=0
        ),
        name="local_attention",
    )(queries, keys, values)


def route_kernel(capacity, per_device, experts, me, ids_column, ids_row, slots_column, slots_row):
    rows = ids_column.shape[0]
    one, zero = jnp.float32(1.0), jnp.float32(0.0)
    before = lax.broadcasted_iota(jnp.int32, (rows, rows), 0) >= lax.broadcasted_iota(jnp.int32, (rows, rows), 1)
    after = lax.broadcasted_iota(jnp.int32, (rows, rows), 0) <= lax.broadcasted_iota(jnp.int32, (rows, rows), 1)
    lower = jnp.where(before, one, zero).astype(jnp.bfloat16)
    upper = jnp.where(after, one, zero).astype(jnp.bfloat16)

    def place(ids, matches, running, axis):
        rank = (jnp.sum(matches * running, axis=axis, keepdims=True) - 1.0).astype(jnp.int32)
        owner = ids // per_device
        return ((owner ^ me[0]) * per_device + ids % per_device) * capacity + rank

    column = ids_column[...]
    matches = jnp.where(column == lax.broadcasted_iota(jnp.int32, (rows, experts), 1), one, zero)
    running = jnp.dot(lower, matches.astype(jnp.bfloat16), preferred_element_type=jnp.float32)
    slots_column[...] = place(column, matches, running, 1)
    row = ids_row[...]
    matches = jnp.where(row == lax.broadcasted_iota(jnp.int32, (experts, rows), 0), one, zero)
    running = jnp.dot(matches.astype(jnp.bfloat16), upper, preferred_element_type=jnp.float32)
    slots_row[...] = place(row, matches, running, 0)


def route(expert_ids, capacity, per_device, experts):
    rows = expert_ids.shape[0]
    me = lax.axis_index("seq").astype(jnp.int32).reshape(1)
    column = pl.BlockSpec((rows, 1), lambda i: (0, 0))
    row = pl.BlockSpec((1, rows), lambda i: (0, 0))
    return pl.pallas_call(
        functools.partial(route_kernel, capacity, per_device, experts),
        grid=(1,),
        in_specs=[pl.BlockSpec(memory_space=pltpu.SMEM), column, row],
        out_specs=[column, row],
        out_shape=[jax.ShapeDtypeStruct((rows, 1), jnp.int32), jax.ShapeDtypeStruct((1, rows), jnp.int32)],
        compiler_params=pltpu.CompilerParams(vmem_limit_bytes=32 * MIB),
        cost_estimate=pl.CostEstimate(
            flops=4 * rows * rows * experts, bytes_accessed=16 * rows, transcendentals=0
        ),
        name="route",
    )(me, expert_ids, expert_ids.reshape(1, rows))


def earlier_states(state, sent):
    size = lax.axis_size("seq")
    me = lax.axis_index("seq")
    prefix = jnp.zeros_like(state)
    total = state
    reach = 1
    while reach < size:
        radix = min(RADIX, size // reach)
        digit = (me // reach) % radix
        gained = jnp.zeros_like(state)
        lower = jnp.zeros_like(state)
        for step in range(1, radix):
            pairs = [(i, i + ((((i // reach) % radix) ^ step) - (i // reach) % radix) * reach) for i in range(size)]
            got = lax.ppermute(sent, "seq", pairs).astype(jnp.float32)
            gained = gained + got
            lower = lower + jnp.where((digit ^ step) < digit, got, 0.0)
        prefix = prefix + lower
        total = total + gained
        sent = total.astype(jnp.bfloat16)
        reach *= radix
    return prefix


def runs_of(partners):
    runs = []
    for partner in partners:
        if runs and sum(runs[-1]) == partner and runs[-1][1] < 4:
            runs[-1] = (runs[-1][0], runs[-1][1] + 1)
        else:
            runs.append((partner, 1))
    return runs


def sort_run(held, slots, run, outs, message):
    first, count = run
    place = first * message + lax.broadcasted_iota(jnp.int32, (count * message, held.shape[0]), 0)
    chosen = jnp.where(place == slots[...], 1.0, 0.0).astype(jnp.bfloat16)
    found = jnp.dot(chosen, held[...], preferred_element_type=jnp.float32).astype(jnp.bfloat16)
    for index, out in enumerate(outs):
        out[...] = found[index * message : (index + 1) * message]


def norm_kernel(head_width, lanes, chunks, partners, message, carried, gain, slots, queries, mixed, normed, *rest):
    outs, held = rest[:-1], rest[-1]
    step = pl.program_id(0)

    @pl.when(step < chunks)
    def _():
        rows, width = queries.shape
        query = queries[...]
        parts = []
        square = jnp.zeros((rows, 1), jnp.float32)
        for group in range(width // lanes):
            at = slice(group * lanes, (group + 1) * lanes)
            moved = spread(carried[:, at], head_width).astype(jnp.bfloat16)
            part = mixed[:, at] + jnp.dot(query[:, at], moved, preferred_element_type=jnp.float32)
            square = square + jnp.sum(part * part, axis=1, keepdims=True)
            parts.append(part)
        scale = lax.rsqrt(square / width + epsilon)
        start = pl.multiple_of(step * rows, rows)
        for group, part in enumerate(parts):
            at = slice(group * lanes, (group + 1) * lanes)
            final = (part * scale * gain[:, at]).astype(jnp.bfloat16)
            normed[:, at] = final
            held[pl.ds(start, rows), at] = final

    done = 0
    for index, run in enumerate(runs_of(partners)):

        @pl.when(step == chunks + index)
        def _(run=run, done=done):
            sort_run(held, slots, run, outs[done : done + run[1]], message)

        done += run[1]


def norm_and_sort(queries, mixed, carried, gain, slots, partners, message, head_width, lanes):
    rows, width = queries.shape
    chunk = tile_of(rows, 256)
    chunks = rows // chunk
    whole = lambda shape: pl.BlockSpec(shape, lambda i: (0, 0))
    by_chunk = pl.BlockSpec((chunk, width), lambda i: (jnp.minimum(i, chunks - 1), 0))
    return pl.pallas_call(
        functools.partial(norm_kernel, head_width, lanes, chunks, partners, message),
        grid=(chunks + len(runs_of(partners)),),
        in_specs=[whole(carried.shape), whole(gain.shape), whole(slots.shape), by_chunk, by_chunk],
        out_specs=[by_chunk] + [whole((message, width))] * len(partners),
        out_shape=[jax.ShapeDtypeStruct((rows, width), jnp.bfloat16)]
        + [jax.ShapeDtypeStruct((message, width), jnp.bfloat16)] * len(partners),
        scratch_shapes=[pltpu.VMEM((rows, width), jnp.bfloat16)],
        compiler_params=pltpu.CompilerParams(vmem_limit_bytes=32 * MIB),
        cost_estimate=pl.CostEstimate(
            flops=2 * rows * width * (len(partners) * message + lanes),
            bytes_accessed=12 * rows * width,
            transcendentals=0,
        ),
        name="norm_and_sort",
    )(carried, gain, slots, queries, mixed)


def sort_kernel(partners, message, slots, normed, *outs):
    done = 0
    for run in runs_of(partners):
        sort_run(normed, slots, run, outs[done : done + run[1]], message)
        done += run[1]


def sort_rows(normed, slots, partners, message):
    rows, width = normed.shape
    return pl.pallas_call(
        functools.partial(sort_kernel, partners, message),
        out_shape=[jax.ShapeDtypeStruct((message, width), jnp.bfloat16)] * len(partners),
        compiler_params=pltpu.CompilerParams(vmem_limit_bytes=32 * MIB),
        cost_estimate=pl.CostEstimate(
            flops=2 * rows * width * len(partners) * message,
            bytes_accessed=2 * (rows + len(partners) * message) * width,
            transcendentals=0,
        ),
        name="sort_rows",
    )(slots, normed)


def pieces(arrays, message, capacity, expert):
    return [
        (index, start + expert * capacity)
        for index, array in enumerate(arrays)
        for start in range(0, array.shape[0], message)
    ]


def expert_kernel(capacity, per_device, count, first, second, after, *rest):
    arrays, outs, held, total = rest[:count], rest[count : 2 * count], rest[-2], rest[-1]
    expert, step = pl.program_id(0), pl.program_id(1)
    message = capacity * per_device
    for own in range(per_device):

        @pl.when((expert == own) & (step == 0))
        def _(own=own):
            for place, (index, start) in enumerate(pieces(arrays, message, capacity, own)):
                held[place * capacity : (place + 1) * capacity] = arrays[index][start : start + capacity]

    hidden = jnp.dot(held[...], first[0], preferred_element_type=jnp.float32)
    hidden = jnp.maximum(hidden, 0.0).astype(jnp.bfloat16)
    added = jnp.dot(hidden, second[0], preferred_element_type=jnp.float32)

    @pl.when(step == 0)
    def _():
        total[...] = added

    @pl.when(step > 0)
    def _():
        total[...] += added

    for own in range(per_device):

        @pl.when((expert == own) & (step == pl.num_programs(1) - 1))
        def _(own=own):
            for place, (index, start) in enumerate(pieces(arrays, message, capacity, own)):
                outs[index][start : start + capacity] = total[place * capacity : (place + 1) * capacity].astype(
                    jnp.bfloat16
                )


def run_experts(arrays, w_in, w_out, capacity, after):
    per_device, width, hidden = w_in.shape
    tile = tile_of(hidden, 768)
    rows = sum(array.shape[0] for array in arrays) // per_device
    whole = [pl.BlockSpec(array.shape, lambda e, f: (0, 0)) for array in arrays]
    return pl.pallas_call(
        functools.partial(expert_kernel, capacity, per_device, len(arrays)),
        grid=(per_device, hidden // tile),
        in_specs=[
            pl.BlockSpec((1, width, tile), lambda e, f: (e, 0, f)),
            pl.BlockSpec((1, tile, width), lambda e, f: (e, f, 0)),
            ANY,
        ]
        + whole,
        out_specs=whole,
        out_shape=[jax.ShapeDtypeStruct(array.shape, jnp.bfloat16) for array in arrays],
        scratch_shapes=[pltpu.VMEM((rows, width), jnp.bfloat16), pltpu.VMEM((rows, width), jnp.float32)],
        compiler_params=pltpu.CompilerParams(vmem_limit_bytes=40 * MIB),
        cost_estimate=pl.CostEstimate(
            flops=4 * per_device * rows * width * hidden,
            bytes_accessed=4 * per_device * width * (rows + hidden),
            transcendentals=0,
        ),
        name="experts",
    )(w_in, w_out, after, *arrays)


def combine_kernel(partners, message, slots, base, *rest):
    returned, out = rest[:-1], rest[-1]
    total = base[...].astype(jnp.float32)
    done = 0
    for first, count in runs_of(partners):
        found = jnp.concatenate([array[...] for array in returned[done : done + count]], axis=0)
        place = first * message + lax.broadcasted_iota(jnp.int32, (base.shape[0], found.shape[0]), 1)
        chosen = jnp.where(place == slots[...], 1.0, 0.0).astype(jnp.bfloat16)
        total = total + jnp.dot(chosen, found, preferred_element_type=jnp.float32)
        done += count
    out[...] = total.astype(jnp.bfloat16)


def combine(base, returned, slots, partners):
    rows, width = base.shape
    message = returned[0].shape[0]
    chunk = tile_of(rows, 256)
    by_chunk = pl.BlockSpec((chunk, width), lambda i: (i, 0))
    return pl.pallas_call(
        functools.partial(combine_kernel, partners, message),
        grid=(rows // chunk,),
        in_specs=[pl.BlockSpec((chunk, 1), lambda i: (i, 0)), by_chunk]
        + [pl.BlockSpec(array.shape, lambda i: (0, 0)) for array in returned],
        out_specs=by_chunk,
        out_shape=jax.ShapeDtypeStruct((rows, width), jnp.bfloat16),
        compiler_params=pltpu.CompilerParams(vmem_limit_bytes=32 * MIB),
        cost_estimate=pl.CostEstimate(
            flops=2 * rows * width * message * len(partners), bytes_accessed=8 * rows * width, transcendentals=0
        ),
        name="combine",
    )(slots, base, *returned)


def shards(queries, keys, values, norm_gain, expert_ids, w_in, w_out):
    rows, width = queries.shape
    head_width = width // HEADS
    lanes = head_width * tile_of(HEADS, max(1, 256 // head_width))
    seq_count = lax.axis_size("seq")
    half, quarter = seq_count // 2, seq_count // 4
    per_device = w_in.shape[0]
    capacity = max(2, 3 * rows // (2 * per_device * seq_count))
    capacity = -(-capacity // 16) * 16
    message = per_device * capacity
    early = [*range(half + quarter, seq_count), *range(quarter, half)]
    late = [*range(half, half + quarter), *range(quarter)]

    def exchange(arrays, partners):
        return [
            lax.ppermute(array, "seq", [(i, i ^ partner) for i in range(seq_count)]) if partner else array
            for array, partner in zip(arrays, partners)
        ]

    state, sent = block_states(keys, values, head_width, lanes)
    carried = earlier_states(state, sent)
    mixed = local_attention(queries, keys, values, head_width, lanes)
    slots_column, slots_row = route(expert_ids, capacity, per_device, per_device * seq_count)
    normed, *first = norm_and_sort(
        queries, mixed, carried, norm_gain.reshape(1, width), slots_row, early, message, head_width, lanes
    )
    second = sort_rows(normed, slots_row, late, message)
    first = exchange(first, early)
    second = exchange(second, late)
    first = exchange(run_experts(first, w_in, w_out, capacity, slots_row), early)
    second = exchange(run_experts(second, w_in, w_out, capacity, first[-1]), late)
    out = combine(normed, first, slots_column, early)
    return combine(out, second, slots_column, late)


def solution(mesh):
    in_specs = (
        P(("dp", "seq"), None),
        P(("dp", "seq"), None),
        P(("dp", "seq"), None),
        P(),
        P(("dp", "seq"), None),
        P(("dp", "seq"), None, None),
        P(("dp", "seq"), None, None),
    )
    out_specs = P(("dp", "seq"), None)
    return jax.shard_map(shards, mesh=mesh, in_specs=in_specs, out_specs=out_specs, check_vma=False)
```
